32 devices in a mesh: groups: 2 (over x), lat: 16 (over z, y, core).
Axes of the slice: x: 2, y: 2, z: 4, core: 2. Of those that a mesh axis runs over, the one named last changes fastest.
Arguments:
- grid_latent: bfloat16 [16384, 512], P(('groups', 'lat')), parts along dimension 0, may hold values from -6 to 6
- mesh_latent: bfloat16 [16384, 512], P(('groups', 'lat')), parts along dimension 0, may hold values from -6 to 6
- g2m_edge: bfloat16 [48, 512, 512], P('lat'), may hold values from -6 to 6
- g2m_sender: int32 [48, 512], P('lat'), may hold values from 0 to 511
- g2m_receiver: int32 [48, 512], P('lat'), may hold values from 0 to 512, as said below
- fine_edge: bfloat16 [16384, 512], P('lat'), may hold values from -6 to 6
- fine_sender: int32 [16384], P('lat'), may hold values from 0 to 575
- fine_receiver: int32 [16384], P('lat'), may hold values from 0 to 511
- coarse_edge: bfloat16 [256, 8, 512], P('lat'), may hold values from -6 to 6
- coarse_sender: int32 [256, 8], P('lat'), may hold values from 0 to 511
- coarse_receiver: int32 [256, 8], P('lat'), may hold values from 0 to 512, as said below
- enc_edge_in: bfloat16 [1536, 512], replicated, may hold values from -0.15625 to 0.15625
- enc_edge_out: bfloat16 [512, 512], replicated, may hold values from -0.25 to 0.25
- enc_edge_par: float32 [3, 512], replicated, may hold values from -1.5 to 1.5
- enc_node_in: bfloat16 [1024, 512], replicated, may hold values from -0.1875 to 0.1875
- enc_node_out: bfloat16 [512, 512], replicated, may hold values from -0.25 to 0.25
- enc_node_par: float32 [3, 512], replicated, may hold values from -1.5 to 1.5
- proc_edge_in: bfloat16 [1536, 512], replicated, may hold values from -0.15625 to 0.15625
- proc_edge_out: bfloat16 [512, 512], replicated, may hold values from -0.25 to 0.25
- proc_edge_par: float32 [3, 512], replicated, may hold values from -1.5 to 1.5
- proc_node_in: bfloat16 [1024, 512], replicated, may hold values from -0.1875 to 0.1875
- proc_node_out: bfloat16 [512, 512], replicated, may hold values from -0.25 to 0.25
- proc_node_par: float32 [3, 512], replicated, may hold values from -1.5 to 1.5
Outputs:
- mesh_out: bfloat16 [16384, 512], P(('groups', 'lat')), parts along dimension 0
The draws below stay inside these ranges and needn't reach their ends.
There are 2 independent parts, one for each index of `groups`. The reference program is written for one: setup_inputs(seed, part) draws one part's arguments, and reference() takes and returns one part's arrays. A program takes and returns all parts, laid end to end along the dimension named above; an argument that names none is the same for every part. Nothing has to cross between parts.
Inputs may be any that keep to these rules, and one draw needn't show every extreme that they name: `g2m_receiver`: the value 512 marks an empty slot; rows whose source device d - j + 1 lies outside 0 to 15 are empty. `coarse_receiver`: entries for a receiving device d lie in rows d * 16 to d * 16 + 15; the value 512 marks an empty slot; pairs of devices more than 8 apart have only empty slots.
All inputs are finite; a program needn't handle non-finite values.
Results may differ from the reference program's by a relative error of at most 0.007.
Values may be sent and summed in bfloat16 or wider, within the bound.
A program may use at most 128 MiB of HBM per device.

```python
import jax
import jax.numpy as jnp
from jax import lax

D = 512
G_DEV = 512
M_DEV = 512
CAP = 512
MCAP = 8
BR = 32
F_DEV = 1024
PAIRS = 256
GRID = 8192
MESH = 8192
FINE = 16384
N_LAT = 16


def fill_threshold(target):
    polar_tilt = jnp.abs(2 * target - (N_LAT - 1))
    return 400 + 500 * polar_tilt * polar_tilt // max((N_LAT - 1) ** 2, 1)


def draw_g2m_receiver(key, part):
    key = jax.random.fold_in(key, 3)
    key_fill, key_node = jax.random.split(key)
    rows_all = 3 * N_LAT
    row_ids = jnp.arange(rows_all, dtype=jnp.int32)[:, None]
    target = row_ids // 3
    offset = row_ids % 3
    source = target - offset + 1
    valid = (source >= 0) & (source < N_LAT)
    slot_index = jnp.arange(CAP, dtype=jnp.int32)[None, :]
    rolled = jax.random.randint(key_fill, (rows_all, CAP), 0, 1000)
    filled = (rolled < fill_threshold(target)) | (slot_index == 0)
    filled = filled & valid
    mesh_index = jax.random.randint(key_node, (rows_all, CAP), 0, M_DEV)
    return jnp.where(filled, mesh_index, M_DEV).astype(jnp.int32)


def draw_coarse_receiver(key, part):
    key = jax.random.fold_in(key, 5)
    key_fill, key_node = jax.random.split(key)
    rows_all = N_LAT * N_LAT
    row_ids = jnp.arange(rows_all, dtype=jnp.int32)[:, None]
    target = row_ids // N_LAT
    source = row_ids % N_LAT
    apart = jnp.abs(source - target)
    reach = apart <= N_LAT // 2
    slot_index = jnp.arange(MCAP, dtype=jnp.int32)[None, :]
    rolled = jax.random.randint(key_fill, (rows_all, MCAP), 0, 1000)
    forced = (slot_index == 0) & ((apart == N_LAT // 2) | (apart <= 1))
    filled = (rolled < fill_threshold(target)) | forced
    filled = filled & reach
    filled = filled & jnp.logical_not((source == (target + 1) % N_LAT) & (slot_index == MCAP - 1))
    mesh_index = jax.random.randint(key_node, (rows_all, MCAP), 0, M_DEV)
    return jnp.where(filled, mesh_index, M_DEV).astype(jnp.int32)


def shape_params(spread_raw):
    return jnp.stack([spread_raw[0] * 1.5, 1.0 + 0.45 * spread_raw[1], spread_raw[2] * 0.8]).astype(jnp.float32)


def draw_enc_edge_par(key, part):
    key = jax.random.fold_in(key, 11)
    spread_raw = jnp.clip(0.5 * jax.random.normal(key, (3, D), jnp.float32), -1.0, 1.0)
    return shape_params(spread_raw)


def draw_enc_node_par(key, part):
    key = jax.random.fold_in(key, 13)
    spread_raw = jnp.clip(0.5 * jax.random.normal(key, (3, D), jnp.float32), -1.0, 1.0)
    return shape_params(spread_raw)


def draw_proc_edge_par(key, part):
    key = jax.random.fold_in(key, 17)
    spread_raw = jnp.clip(0.5 * jax.random.normal(key, (3, D), jnp.float32), -1.0, 1.0)
    return shape_params(spread_raw)


def draw_proc_node_par(key, part):
    key = jax.random.fold_in(key, 19)
    spread_raw = jnp.clip(0.5 * jax.random.normal(key, (3, D), jnp.float32), -1.0, 1.0)
    return shape_params(spread_raw)


def plant(values, key, smallest, high):
    shape = values.shape
    index_at = [jax.random.randint(jax.random.fold_in(key, axis), (), 0, shape[axis]) for axis in range(len(shape))]
    values = values.at[tuple(index_at)].set(smallest)
    longest = shape.index(max(shape))
    index_at[longest] = (index_at[longest] + 1) % shape[longest]
    return values.at[tuple(index_at)].set(high)


def block_levels(own_key, shape, pieces, smallest, top_value):
    factor_of = 1.0
    for dim, parts in pieces:
        draws = jax.random.uniform(jax.random.fold_in(jax.random.fold_in(own_key, 6), dim), (parts,), jnp.float32, smallest / len(pieces), top_value / len(pieces))
        factor_of = factor_of * jnp.repeat(jnp.exp(draws), shape[dim] // parts).reshape((-1,) + (1,) * (len(shape) - 1 - dim))
    return factor_of


def normal_values(own_key, extent, width, limit, pieces=(), held_as=jnp.bfloat16):
    level = block_levels(own_key, extent, pieces, -0.22, 0.18) if pieces else 1.0
    entries = jax.random.normal(own_key, extent, jnp.float32) * width * level
    return jnp.minimum(jnp.maximum(entries, -limit), limit).astype(held_as)


def setup_inputs(seed: int = 0, part: int = 0) -> dict:
    key_list = jax.random.split(jax.random.key(seed), 24)
    part_keys = jax.random.split(jax.random.fold_in(key_list[23], part), 24)
    return {
        "grid_latent": normal_values(part_keys[0], (GRID, D), 1.0, 6.0, ((0, 16),)),
        "mesh_latent": normal_values(part_keys[1], (MESH, D), 1.0, 6.0, ((0, 16),)),
        "g2m_edge": normal_values(key_list[2], (3 * N_LAT, CAP, D), 1.0, 6.0, ((0, 16),)),
        "g2m_sender": plant(jax.random.randint(key_list[3], (3 * N_LAT, CAP), 0, G_DEV), jax.random.fold_in(key_list[3], 1), 0, G_DEV - 1).astype(jnp.int32),
        "g2m_receiver": draw_g2m_receiver(jax.random.fold_in(key_list[23], 71), part),
        "fine_edge": normal_values(key_list[5], (FINE, D), 1.0, 6.0, ((0, 16),)),
        "fine_sender": plant(jax.random.randint(key_list[6], (FINE,), 0, M_DEV + 2 * BR), jax.random.fold_in(key_list[6], 1), 0, (M_DEV + 2 * BR) - 1).astype(jnp.int32),
        "fine_receiver": plant(jax.random.randint(key_list[7], (FINE,), 0, M_DEV), jax.random.fold_in(key_list[7], 1), 0, M_DEV - 1).astype(jnp.int32),
        "coarse_edge": normal_values(key_list[8], (PAIRS, MCAP, D), 1.0, 6.0, ((0, 16),)),
        "coarse_sender": plant(jax.random.randint(key_list[9], (PAIRS, MCAP), 0, M_DEV), jax.random.fold_in(key_list[9], 1), 0, M_DEV - 1).astype(jnp.int32),
        "coarse_receiver": draw_coarse_receiver(jax.random.fold_in(key_list[23], 71), part),
        "enc_edge_in": normal_values(key_list[11], (3 * D, D), (3 * D) ** -0.5, 0.15625),
        "enc_edge_out": normal_values(key_list[12], (D, D), D ** -0.5, 0.25),
        "enc_edge_par": draw_enc_edge_par(jax.random.fold_in(key_list[23], 71), part),
        "enc_node_in": normal_values(key_list[14], (2 * D, D), (2 * D) ** -0.5, 0.1875),
        "enc_node_out": normal_values(key_list[15], (D, D), D ** -0.5, 0.25),
        "enc_node_par": draw_enc_node_par(jax.random.fold_in(key_list[23], 71), part),
        "proc_edge_in": normal_values(key_list[17], (3 * D, D), (3 * D) ** -0.5, 0.15625),
        "proc_edge_out": normal_values(key_list[18], (D, D), D ** -0.5, 0.25),
        "proc_edge_par": draw_proc_edge_par(jax.random.fold_in(key_list[23], 71), part),
        "proc_node_in": normal_values(key_list[20], (2 * D, D), (2 * D) ** -0.5, 0.1875),
        "proc_node_out": normal_values(key_list[21], (D, D), D ** -0.5, 0.25),
        "proc_node_par": draw_proc_node_par(jax.random.fold_in(key_list[23], 71), part),
    }


def layer_norm(values, params):
    average = lax.optimization_barrier(jnp.mean(values, axis=-1, keepdims=True))
    centred = values - average
    spread = lax.optimization_barrier(jnp.mean(centred * centred, axis=-1, keepdims=True))
    return centred * lax.rsqrt(spread + 1e-05) * params[1] + params[2]

def edge_message(preact, w_out, params):
    hidden = jax.nn.silu(preact + params[0]).astype(jnp.bfloat16)
    output = jnp.dot(hidden, w_out, preferred_element_type=jnp.float32)
    return layer_norm(output, params).astype(jnp.bfloat16)

def node_update(latent, summed, w_in, w_out, params):
    breadth = latent.shape[1]
    preact = jnp.dot(latent, w_in[:breadth], preferred_element_type=jnp.float32)
    preact = preact + jnp.dot(summed.astype(jnp.bfloat16), w_in[breadth:], preferred_element_type=jnp.float32)
    hidden = jax.nn.silu(preact + params[0]).astype(jnp.bfloat16)
    output = layer_norm(jnp.dot(hidden, w_out, preferred_element_type=jnp.float32), params)
    return (latent.astype(jnp.float32) + output).astype(jnp.bfloat16)

def take_rows(lookup, indices):
    present = indices < lookup.shape[0]
    picked = jnp.take(lookup, jnp.minimum(indices, lookup.shape[0] - 1), axis=0).astype(jnp.float32)
    return jnp.where(present[:, None], picked, 0.0)

def reference(grid_latent, mesh_latent, g2m_edge, g2m_sender, g2m_receiver, fine_edge, fine_sender, fine_receiver, coarse_edge, coarse_sender, coarse_receiver, enc_edge_in, enc_edge_out, enc_edge_par, enc_node_in, enc_node_out, enc_node_par, proc_edge_in, proc_edge_out, proc_edge_par, proc_node_in, proc_node_out, proc_node_par):
    band_count = N_LAT
    grid_table = grid_latent.reshape(band_count, G_DEV, D)
    mesh_table = mesh_latent.reshape(band_count, M_DEV, D)
    edge_four = g2m_edge.reshape(band_count, 3, CAP, D)
    sender_three = g2m_sender.reshape(band_count, 3, CAP)
    receiver_three = g2m_receiver.reshape(band_count, 3, CAP)
    band_ids = jnp.arange(band_count, dtype=jnp.int32)
    offsets = jnp.arange(3, dtype=jnp.int32)
    recv_table = jnp.dot(mesh_latent, enc_edge_in[2 * D:], preferred_element_type=jnp.float32).astype(jnp.bfloat16).reshape(band_count, M_DEV, D)

    def encode(device):
        sources = jnp.clip(device - offsets + 1, 0, band_count - 1).astype(jnp.int32)
        edge_rows = edge_four[sources, offsets].reshape(-1, D)
        senders = sender_three[sources, offsets]
        grid_rows = grid_table[sources[:, None], senders].reshape(-1, D)
        edge_term = (jnp.dot(edge_rows, enc_edge_in[:D], preferred_element_type=jnp.float32) + jnp.dot(grid_rows, enc_edge_in[D:2 * D], preferred_element_type=jnp.float32)).astype(jnp.bfloat16)
        receivers = receiver_three[device].reshape(-1)
        preact = edge_term.astype(jnp.float32) + take_rows(recv_table[device], receivers)
        message = edge_message(preact, enc_edge_out, enc_edge_par)
        summed = jax.ops.segment_sum(message.astype(jnp.float32), receivers, num_segments=M_DEV + 1)[:M_DEV]
        return node_update(mesh_table[device], summed, enc_node_in, enc_node_out, enc_node_par)
    mesh_enc = lax.map(encode, band_ids)
    flat_enc = mesh_enc.reshape(-1, D)
    send_proj = jnp.dot(flat_enc, proc_edge_in[D:2 * D], preferred_element_type=jnp.float32).astype(jnp.bfloat16)
    recv_proj = jnp.dot(flat_enc, proc_edge_in[2 * D:], preferred_element_type=jnp.float32).astype(jnp.bfloat16).reshape(band_count, M_DEV, D)
    rim_zeros = jnp.zeros((BR, D), jnp.bfloat16)
    padded = jnp.concatenate([rim_zeros, send_proj, rim_zeros], axis=0)
    send_table = send_proj.reshape(band_count, M_DEV, D)
    fine_three = fine_edge.reshape(band_count, F_DEV, D)
    fine_senders = fine_sender.reshape(band_count, F_DEV)
    fine_receivers = fine_receiver.reshape(band_count, F_DEV)
    coarse_four = coarse_edge.reshape(band_count, band_count, MCAP, D)
    coarse_senders = coarse_sender.reshape(band_count, band_count, MCAP)
    coarse_receivers = coarse_receiver.reshape(band_count, band_count, MCAP)

    def process(device):
        near_rows = jnp.take(padded, device * M_DEV + fine_senders[device], axis=0)
        far_rows = send_table[band_ids[:, None], jnp.take(coarse_senders, device, axis=1)].reshape(-1, D)
        edge_rows = jnp.concatenate([fine_three[device], coarse_four[device].reshape(-1, D)], axis=0)
        send_terms = jnp.concatenate([near_rows, far_rows], axis=0).astype(jnp.float32)
        receivers = jnp.concatenate([fine_receivers[device], coarse_receivers[device].reshape(-1)], axis=0)
        preact = jnp.dot(edge_rows, proc_edge_in[:D], preferred_element_type=jnp.float32) + send_terms + take_rows(recv_proj[device], receivers)
        message = edge_message(preact, proc_edge_out, proc_edge_par)
        summed = jax.ops.segment_sum(message.astype(jnp.float32), receivers, num_segments=M_DEV + 1)[:M_DEV]
        return node_update(mesh_enc[device], summed, proc_node_in, proc_node_out, proc_node_par)
    return lax.map(process, band_ids).reshape(-1, D)
```

```python
import functools

import jax
import jax.numpy as jnp
from jax import lax
from jax.experimental import pallas as pl
from jax.experimental.pallas import tpu as pltpu
from jax.sharding import PartitionSpec as P

BR = 32
LANES = 128
CHUNK = 128
MESH = pl.DeviceIdType.MESH
F32 = jnp.float32
BF16 = jnp.bfloat16


def dot(a, b):
    return jnp.dot(a, b, preferred_element_type=F32)


def silu(x):
    half = 0.5 * x
    return half + half * jnp.tanh(half)


def normed(values, par):
    average = jnp.mean(values, axis=-1, keepdims=True)
    centred = values - average
    spread = jnp.mean(centred * centred, axis=-1, keepdims=True)
    return centred * lax.rsqrt(spread + 1e-05) * par[1:2, :] + par[2:3, :]


def mlp(preact, w_out, par):
    hidden = silu(preact + par[0:1, :]).astype(BF16)
    return normed(dot(hidden, w_out[...]), par)


def gather_matrix(row, extent):
    slots = row.shape[1]
    column = jnp.transpose(jnp.broadcast_to(row, (LANES, slots)))
    lane = lax.broadcasted_iota(jnp.int32, (slots, LANES), 1)
    pieces = [
        jnp.where(column == lane + start, 1.0, 0.0).astype(BF16)
        for start in range(0, extent, LANES)
    ]
    return pieces[0] if len(pieces) == 1 else jnp.concatenate(pieces, axis=1)


def sum_matrix(row, extent):
    slots = row.shape[1]
    node = lax.broadcasted_iota(jnp.int32, (extent, slots), 0)
    return jnp.where(node == row, 1.0, 0.0).astype(BF16)


NAMES = (
    "grid", "mesh", "g_edge", "g_send", "g_recv", "f_edge", "f_send", "f_recv", "c_edge", "c_send", "c_recv",
    "ee_in", "ee_out", "ee_par", "en_in", "en_out", "en_par",
    "pe_in", "pe_out", "pe_par", "pn_in", "pn_out", "pn_par",
)
ORDER = (
    "grid", "ee_in", "g_send", "g_edge", "mesh", "g_recv", "ee_par", "ee_out", "en_in", "f_edge", "pe_in",
    "c_edge", "f_send", "f_recv", "c_send", "c_recv", "en_par", "en_out", "pe_par", "pe_out",
    "pn_in", "pn_out", "pn_par",
)


def kernel(n, *refs):
    count = len(NAMES)
    sources = dict(zip(NAMES, refs[:count]))
    out_ref = refs[count]
    held = dict(zip(NAMES, refs[count + 1 : 2 * count + 1]))
    (
        g_table, r_table, leaving, arrived, r_terms, e_sum, acc, f_pre, c_pre, n_pre, enc, payload, proj,
        s_own, s_rim, s_recv, t_fine, s_far, s_crecv, t_far, rim, far_out, far_in,
        in_sem, halo_send, halo_recv, rim_send, rim_recv, far_send, far_recv,
    ) = refs[2 * count + 1 :]
    me = lax.axis_index("lat")
    reach = n // 2
    width = enc.shape[1]
    nodes = enc.shape[0]
    cap = leaving.shape[1]
    fine = f_pre.shape[0]
    far_rows = c_pre.shape[0]

    copies = {
        name: pltpu.make_async_copy(sources[name], held[name], in_sem.at[index])
        for index, name in enumerate(NAMES)
    }
    for name in ORDER:
        copies[name].start()

    rim[...] = jnp.zeros_like(rim)
    far_in[...] = jnp.zeros_like(far_in)

    @pl.when(me == n - 1)
    def _():
        arrived[0] = jnp.zeros((cap, width), BF16)

    @pl.when(me == 0)
    def _():
        arrived[1] = jnp.zeros((cap, width), BF16)

    barrier = pltpu.get_barrier_semaphore()

    def greet(step, carry):
        @pl.when(me - step >= 0)
        def _():
            pl.semaphore_signal(barrier, inc=1, device_id={"lat": me - step}, device_id_type=MESH)

        @pl.when(me + step < n)
        def _():
            pl.semaphore_signal(barrier, inc=1, device_id={"lat": me + step}, device_id_type=MESH)

        return carry

    lax.fori_loop(1, reach + 1, greet, 0)

    def halo(side, chunk):
        peer = me - 1 if side == 0 else me + 1
        rows = pl.ds(chunk * CHUNK, CHUNK)
        return pltpu.make_async_remote_copy(
            src_ref=leaving.at[side, rows],
            dst_ref=arrived.at[side, rows],
            send_sem=halo_send.at[side, chunk],
            recv_sem=halo_recv.at[side, chunk],
            device_id={"lat": peer},
            device_id_type=MESH,
        )

    def sends(side):
        return me > 0 if side == 0 else me < n - 1

    def receives(side):
        return me < n - 1 if side == 0 else me > 0

    chunks = cap // CHUNK

    copies["grid"].wait()
    copies["ee_in"].wait()
    w = held["ee_in"]
    g_table[...] = dot(held["grid"][...], w[width : 2 * width, :]).astype(BF16)
    copies["g_send"].wait()
    copies["g_edge"].wait()
    pl.semaphore_wait(barrier, jnp.minimum(me, reach) + jnp.minimum(n - 1 - me, reach))

    def edge_term(j, chunk):
        rows = slice(chunk * CHUNK, (chunk + 1) * CHUNK)
        chosen = gather_matrix(held["g_send"][j : j + 1, rows], nodes_grid)
        return (dot(held["g_edge"][j, rows, :], w[0:width, :]) + dot(chosen, g_table[...])).astype(BF16)

    nodes_grid = g_table.shape[0]
    for chunk in range(chunks):
        rows = slice(chunk * CHUNK, (chunk + 1) * CHUNK)
        for side in range(2):
            leaving[side, rows, :] = edge_term(2 * side, chunk)

            @pl.when(sends(side))
            def _():
                halo(side, chunk).start()

    copies["mesh"].wait()
    copies["g_recv"].wait()
    r_table[...] = dot(held["mesh"][...], w[2 * width :, :]).astype(BF16)
    copies["ee_par"].wait()
    copies["ee_out"].wait()
    e_par = held["ee_par"][...]
    for j in range(3):
        row = held["g_recv"][j : j + 1, :]
        r_terms[j] = dot(gather_matrix(row, nodes), r_table[...])
        e_sum[j] = sum_matrix(row, nodes)
    total = jnp.zeros((nodes, width), F32)
    for chunk in range(0, chunks, 2):
        rows = slice(chunk * CHUNK, (chunk + 2) * CHUNK)
        term = jnp.concatenate([edge_term(1, chunk), edge_term(1, chunk + 1)], axis=0)
        message = mlp(term.astype(F32) + r_terms[1, rows, :], held["ee_out"], e_par).astype(BF16)
        total = total + dot(e_sum[1, :, rows], message)
    acc[...] = total
    copies["en_in"].wait()
    n_pre[...] = dot(held["mesh"][...], held["en_in"][0:width, :])
    for name in ("f_edge", "pe_in", "c_edge", "f_send", "f_recv", "c_send", "c_recv"):
        copies[name].wait()
    pw = held["pe_in"]
    step = min(fine, 256)
    for start in range(0, fine, step):
        rows = slice(start, start + step)
        f_pre[rows, :] = dot(held["f_edge"][rows, :], pw[0:width, :])
        sender = held["f_send"][0:1, rows]
        s_own[rows, :] = gather_matrix(sender - BR, nodes)
        outer = jnp.where(sender < BR, sender, jnp.where(sender >= nodes + BR, sender - nodes, -1))
        s_rim[rows, :] = gather_matrix(outer, LANES)
        receiver = held["f_recv"][0:1, rows]
        s_recv[rows, :] = gather_matrix(receiver, nodes)
        t_fine[:, rows] = sum_matrix(receiver, nodes)
    far_step = min(far_rows, 256)
    for start in range(0, far_rows, far_step):
        rows = slice(start, start + far_step)
        c_pre[rows, :] = dot(held["c_edge"][rows, :], pw[0:width, :])
        s_far[rows, :] = gather_matrix(held["c_send"][0:1, rows], nodes)
        s_crecv[rows, :] = gather_matrix(held["c_recv"][0:1, rows], nodes)
        t_far[:, rows] = sum_matrix(held["c_recv"][0:1, rows], nodes)
    for name in ("en_par", "en_out", "pe_par", "pe_out", "pn_in", "pn_out", "pn_par"):
        copies[name].wait()

    for chunk in range(chunks):
        rows = slice(chunk * CHUNK, (chunk + 1) * CHUNK)
        for side in range(2):

            @pl.when(receives(side))
            def _():
                halo(side, chunk).wait_recv()

        z = jnp.concatenate(
            [arrived[side, rows, :].astype(F32) + r_terms[2 * side, rows, :] for side in range(2)], axis=0
        )
        message = mlp(z, held["ee_out"], e_par).astype(BF16)
        chosen = jnp.concatenate([e_sum[0, :, rows], e_sum[2, :, rows]], axis=1)
        acc[...] += dot(chosen, message)

    z = n_pre[...] + dot(acc[...].astype(BF16), held["en_in"][width:, :])
    enc[...] = (held["mesh"][...].astype(F32) + mlp(z, held["en_out"], held["en_par"][...])).astype(BF16)

    payload[...] = dot(enc[...], pw[width : 2 * width, :]).astype(BF16)

    def rim_copy(side):
        start = 0 if side == 0 else nodes - BR
        return pltpu.make_async_remote_copy(
            src_ref=payload.at[pl.ds(start, BR)],
            dst_ref=rim.at[pl.ds(BR if side == 0 else 0, BR)],
            send_sem=rim_send.at[side],
            recv_sem=rim_recv.at[side],
            device_id={"lat": me - 1 if side == 0 else me + 1},
            device_id_type=MESH,
        )

    for side in range(2):

        @pl.when(sends(side))
        def _():
            rim_copy(side).start()

    half = width // 2
    slots = far_rows // n
    for start in range(0, far_rows, far_step):
        rows = slice(start, start + far_step)
        picked = dot(s_far[rows, :], payload[...])
        low = picked[:, :half].reshape(far_step // slots, slots, half)
        high = picked[:, half:].reshape(far_step // slots, slots, half)
        far_out[start // slots : (start + far_step) // slots] = jnp.concatenate([low, high], axis=1).astype(BF16)

    def far_copy(slot_out, slot_in, peer):
        return pltpu.make_async_remote_copy(
            src_ref=far_out.at[slot_out],
            dst_ref=far_in.at[slot_in],
            send_sem=far_send.at[slot_out],
            recv_sem=far_recv.at[slot_in],
            device_id={"lat": peer},
            device_id_type=MESH,
        )

    def over_peers(act):
        def body(index, carry):
            distance = reach - index

            @pl.when(me - distance >= 0)
            def _():
                act(me - distance)

            @pl.when(me + distance < n)
            def _():
                act(me + distance)

            return carry

        lax.fori_loop(0, reach, body, 0)

    over_peers(lambda peer: far_copy(peer, me, peer).start())
    far_in[me] = far_out[me]

    proj[...] = dot(enc[...], pw[2 * width :, :]).astype(BF16)
    n_pre[...] = dot(enc[...], held["pn_in"][0:width, :])
    for start in range(0, fine, step):
        rows = slice(start, start + step)
        f_pre[rows, :] += dot(s_own[rows, :], payload[...]) + dot(s_recv[rows, :], proj[...])
    for start in range(0, far_rows, far_step):
        rows = slice(start, start + far_step)
        c_pre[rows, :] += dot(s_crecv[rows, :], proj[...])
    for side in range(2):

        @pl.when(receives(side))
        def _():
            rim_copy(side).wait_recv()

    p_par = held["pe_par"][...]
    total = jnp.zeros((nodes, width), F32)
    for start in range(0, fine, step):
        rows = slice(start, start + step)
        z = f_pre[rows, :] + dot(s_rim[rows, :], rim[...])
        message = mlp(z, held["pe_out"], p_par).astype(BF16)
        total = total + dot(t_fine[:, rows], message)
    over_peers(lambda peer: far_copy(peer, peer, peer).wait_recv())
    for start in range(0, far_rows, far_step):
        rows = slice(start, start + far_step)
        got = far_in[start // slots : (start + far_step) // slots].astype(F32)
        terms = jnp.concatenate(
            [got[:, :slots, :].reshape(far_step, half), got[:, slots:, :].reshape(far_step, half)], axis=1
        )
        message = mlp(c_pre[rows, :] + terms, held["pe_out"], p_par).astype(BF16)
        total = total + dot(t_far[:, rows], message)
    z = n_pre[...] + dot(total.astype(BF16), held["pn_in"][width:, :])
    out_ref[...] = (enc[...].astype(F32) + mlp(z, held["pn_out"], held["pn_par"][...])).astype(BF16)

    for side in range(2):

        @pl.when(sends(side))
        def _():
            for chunk in range(chunks):
                halo(side, chunk).wait_send()
            rim_copy(side).wait_send()

    over_peers(lambda peer: far_copy(peer, me, peer).wait_send())


def per_device(n, *args):
    args = list(args)
    width = args[0].shape[1]
    for index in (6, 7, 9, 10):
        args[index] = args[index].reshape(1, -1)
    args[8] = args[8].reshape(-1, width)
    grid_nodes, nodes, cap = args[0].shape[0], args[1].shape[0], args[2].shape[1]
    fine, far = args[5].shape[0], args[8].shape[0]
    slots = far // n
    chunks = cap // CHUNK
    vmem = pltpu.VMEM
    dma = pltpu.SemaphoreType.DMA
    scratch = [vmem(a.shape, a.dtype) for a in args] + [
        vmem((grid_nodes, width), BF16),
        vmem((nodes, width), BF16),
        vmem((2, cap, width), BF16),
        vmem((2, cap, width), BF16),
        vmem((3, cap, width), F32),
        vmem((3, nodes, cap), BF16),
        vmem((nodes, width), F32),
        vmem((fine, width), F32),
        vmem((far, width), F32),
        vmem((nodes, width), F32),
        vmem((nodes, width), BF16),
        vmem((nodes, width), BF16),
        vmem((nodes, width), BF16),
        vmem((fine, nodes), BF16),
        vmem((fine, LANES), BF16),
        vmem((fine, nodes), BF16),
        vmem((nodes, fine), BF16),
        vmem((far, nodes), BF16),
        vmem((far, nodes), BF16),
        vmem((nodes, far), BF16),
        vmem((LANES, width), BF16),
        vmem((n, 2 * slots, width // 2), BF16),
        vmem((n, 2 * slots, width // 2), BF16),
        dma((len(args),)),
        dma((2, chunks)),
        dma((2, chunks)),
        dma((2,)),
        dma((2,)),
        dma((n,)),
        dma((n,)),
    ]
    return pl.pallas_call(
        functools.partial(kernel, n),
        out_shape=jax.ShapeDtypeStruct((nodes, width), BF16),
        in_specs=[pl.BlockSpec(memory_space=pl.ANY)] * len(args),
        out_specs=pl.BlockSpec(memory_space=vmem),
        scratch_shapes=scratch,
        compiler_params=pltpu.CompilerParams(
            collective_id=0, has_side_effects=True, vmem_limit_bytes=56 * 1024 * 1024
        ),
        cost_estimate=pl.CostEstimate(flops=10**10, bytes_accessed=12 * 10**6, transcendentals=2 * 10**6),
    )(*args)


def solution(mesh):
    in_specs = (
        P(("groups", "lat"), None),
        P(("groups", "lat"), None),
        P("lat", None, None),
        P("lat", None),
        P("lat", None),
        P("lat", None),
        P("lat"),
        P("lat"),
        P("lat", None, None),
        P("lat", None),
        P("lat", None),
    ) + (P(),) * 12
    return jax.shard_map(
        functools.partial(per_device, mesh.shape["lat"]),
        mesh=mesh,
        in_specs=in_specs,
        out_specs=P(("groups", "lat"), None),
        check_vma=False,
    )
```
